128 devices in a mesh: row: 8 (over x, y_hi), col: 16 (over y_lo, z, core).
Axes of the slice: x: 4, y: 4 (y_hi: 2, y_lo: 2; y = y_hi * 2 + y_lo), z: 4, core: 2. Of those that a mesh axis runs over, the one named last changes fastest.
Arguments:
- feat_rows: float32 [8192, 512], P(('row', 'col')), may hold values from -0.6 to 0.6
- feat_cols: float32 [8192, 512], P(('col', 'row')), may hold values from -0.6 to 0.6
- panel_rows: float32 [8192, 1024], P(('row', 'col')), may hold values from -0.6 to 0.6
- panel_cols: float32 [8192, 1024], P(('col', 'row')), may hold values from -0.6 to 0.6
- accumulator: float32 [8192, 8192], P('row', 'col'), may hold values from -1.8 to 1.8
Outputs:
- acc_new: float32 [8192, 8192], P('row', 'col')
- grad_rows: float32 [8192, 512], P(('row', 'col'))
- grad_cols: float32 [8192, 512], P(('col', 'row'))
The draws below stay inside these ranges and needn't reach their ends.
All inputs are finite; a program needn't handle non-finite values.
Results may differ from the reference program's by a relative error of at most 0.00011.
Values sent between devices are 32-bit elements; how exact they have to be, the bound alone decides.
No kernel may reach another device: no remote copies, remote signals or barrier semaphores. Data moves between devices by JAX's collectives and lax.ppermute only.
A program may use at most 64 MiB of HBM per device.

```python
import jax
import jax.numpy as jnp
from jax import lax

F = 512
PANEL = 512
PANELS = 2
NA = 8192
NB = 8192
N_ROW = 8


def steps_of(key, extent, pieces, least, top_value):
    factor_of, own = 1.0, jax.random.fold_in(key, 6)
    for position, parts in pieces:
        heights = jnp.exp(jax.random.uniform(jax.random.fold_in(own, position), (parts,), jnp.float32, least / len(pieces), top_value / len(pieces)))
        factor_of = factor_of * jnp.repeat(heights, extent[position] // parts).reshape([-1 if axis == position else 1 for axis in range(len(extent))])
    return factor_of


def scatter_about(rng, extent, scale, limit, split=(), kind=jnp.bfloat16):
    gain = steps_of(rng, extent, split, -0.22, 0.18) if split else 1.0
    result = jax.random.normal(rng, extent, jnp.float32) * scale * gain
    return jnp.minimum(jnp.maximum(result, -limit), limit).astype(kind)


def setup_inputs(seed: int = 0) -> dict:
    streams_of = jax.random.split(jax.random.key(seed), 6)
    return {
        "feat_rows": scatter_about(streams_of[0], (NA, F), 0.1, 0.6, ((0, 128),), jnp.float32),
        "feat_cols": scatter_about(streams_of[1], (NB, F), 0.1, 0.6, ((0, 128),), jnp.float32),
        "panel_rows": scatter_about(streams_of[2], (NA, PANELS * PANEL), 0.1, 0.6, ((0, 128),), jnp.float32),
        "panel_cols": scatter_about(streams_of[3], (NB, PANELS * PANEL), 0.1, 0.6, ((0, 128),), jnp.float32),
        "accumulator": scatter_about(streams_of[4], (NA, NB), 0.3, 1.8, ((0, 8), (1, 16)), jnp.float32),
    }


decay_rate = 0.125
grad_scale = 0.25


def local_tile(rows_feat, rows_panel, acc_tile, cols_feat, cols_panel):
    grams_tile = acc_tile + jnp.dot(rows_panel, cols_panel.T, precision=lax.Precision.HIGHEST)
    cross_term = jnp.dot(rows_feat, cols_feat.T, precision=lax.Precision.HIGHEST)
    norm_rows = jnp.sum(rows_feat * rows_feat, axis=1)
    norm_cols = jnp.sum(cols_feat * cols_feat, axis=1)
    dist_sq = norm_rows[:, None] + norm_cols[None, :] - 2.0 * cross_term
    kernel = jnp.exp(-decay_rate * dist_sq)
    weights = grams_tile * kernel
    row_term = grad_scale * (jnp.dot(weights, cols_feat, precision=lax.Precision.HIGHEST) - jnp.sum(weights, axis=1)[:, None] * rows_feat)
    col_term = grad_scale * (jnp.dot(weights.T, rows_feat, precision=lax.Precision.HIGHEST) - jnp.sum(weights, axis=0)[:, None] * cols_feat)
    return grams_tile, row_term, col_term


def reference(feat_rows, feat_cols, panel_rows, panel_cols, accumulator):
    blocks = N_ROW
    height = NA // blocks
    rows_feat = feat_rows.reshape(blocks, height, F)
    rows_panel = panel_rows.reshape(blocks, height, PANELS * PANEL)
    acc_blocks = accumulator.reshape(blocks, height, NB)

    def step_fn(totals, inputs):
        feat_blk, panel_blk, acc_blk = inputs
        grams_tile, row_term, col_term = local_tile(feat_blk, panel_blk, acc_blk, feat_cols, panel_cols)
        return totals + col_term, (grams_tile, row_term)

    init = jnp.zeros((NB, F), jnp.float32)
    col_total, outputs = lax.scan(step_fn, init, (rows_feat, rows_panel, acc_blocks))
    acc_new = outputs[0].reshape(NA, NB)
    grad_rows = outputs[1].reshape(NA, F)
    return acc_new, grad_rows, col_total
```

```python
import jax
import jax.numpy as jnp
from jax import lax
from jax.experimental import pallas as pl
from jax.experimental.pallas import tpu as pltpu
from jax.sharding import PartitionSpec as P

decay_rate = 0.125
grad_scale = 0.25

B = 64
F = 512
K = 1024
STEPS = 4
ROWS = 1024
COLS = 512
CHUNK = ROWS // STEPS
SHIFTS = (0, 1, 3, 2)


def col_perm(dy, dz, dc):
    return [(q, (((q // 8) ^ dy) * 8) + (((q // 2 + dz) % 4) * 2) + ((q % 2) ^ dc)) for q in range(16)]


def row_perm(dx, dh):
    return [(r, ((r // 2 + dx) % 4) * 2 + ((r % 2) ^ dh)) for r in range(8)]


def over_col(a, dy=0, dz=0, dc=0):
    return lax.ppermute(a, "col", col_perm(dy, dz, dc))


def over_row(a, dx=0, dh=0):
    return lax.ppermute(a, "row", row_perm(dx, dh))


def split(a):
    hi = a.astype(jnp.bfloat16)
    return hi, (a - hi.astype(jnp.float32)).astype(jnp.bfloat16)


def dot3(ah, al, bh, bl, dims):
    def one(p, q):
        return lax.dot_general(p, q, (dims, ((), ())), preferred_element_type=jnp.float32)

    return one(ah, bh) + (one(ah, bl) + one(al, bh))


NT = ((1,), (1,))
NN = ((1,), (0,))
TN = ((0,), (0,))


def tile_kernel(place, *refs):
    rows = refs[:16]
    cols = refs[16:24]
    acc = refs[24]
    acc_new = refs[25]
    own_out = refs[26:30]
    sib_out = refs[30]
    col_out = refs[31:35]
    rh, rl, rf, ch, cl, cf, nr, nc, row_term, col_term, tsum = refs[35:]
    step = pl.program_id(0)

    @pl.when(step == 0)
    def _():
        for n in range(16):
            at = pl.ds(pl.multiple_of(place[n] * B, B), B)
            piece = rows[n][...]
            hi, lo = split(piece)
            rh[at, :] = hi
            rl[at, :] = lo
            feat = piece[:, :F]
            rf[at, :] = feat
            nr[at, :] = jnp.broadcast_to(jnp.sum(feat * feat, axis=1, keepdims=True), (B, 128))
        for n in range(8):
            at = pl.ds(pl.multiple_of(place[16 + n] * B, B), B)
            piece = cols[n][...]
            hi, lo = split(piece)
            ch[at, :] = hi
            cl[at, :] = lo
            feat = piece[:, :F]
            cf[at, :] = feat
            nc[at, :] = jnp.broadcast_to(jnp.sum(feat * feat, axis=1, keepdims=True), (B, 128))
        col_term[...] = jnp.zeros_like(col_term)
        tsum[...] = jnp.zeros_like(tsum)

    at = pl.ds(pl.multiple_of(step * CHUNK, CHUNK), CHUNK)
    rhc, rlc = rh[at, :], rl[at, :]
    chh, cll = ch[...], cl[...]
    grams = acc[...] + dot3(rhc[:, F:], rlc[:, F:], chh[:, F:], cll[:, F:], NT)
    acc_new[...] = grams
    cross = dot3(rhc[:, :F], rlc[:, :F], chh[:, :F], cll[:, :F], NT)
    nc_row = nc[...].T[0:1, :]
    dist_sq = nr[at, :][:, 0:1] + nc_row - 2.0 * cross
    weights = grams * jnp.exp(-decay_rate * dist_sq)
    wh, wl = split(weights)
    s = jnp.sum(weights, axis=1, keepdims=True)
    row_term[at, :] = grad_scale * (dot3(wh, wl, chh[:, :F], cll[:, :F], NN) - s * rf[at, :])
    col_term[...] += dot3(wh, wl, rhc[:, :F], rlc[:, :F], TN)
    tsum[...] += jnp.broadcast_to(jnp.sum(weights, axis=0, keepdims=True), (8, COLS))

    @pl.when(step == STEPS - 1)
    def _():
        for n in range(4):
            for d in range(2):
                own_out[n][d] = row_term[pl.ds(pl.multiple_of(place[24 + n * 2 + d] * B, B), B), :]
                sib_out[n * 2 + d] = row_term[pl.ds(pl.multiple_of(place[32 + n * 2 + d] * B, B), B), :]
        t = jnp.broadcast_to(tsum[0:1, :], (128, COLS)).T[:, 0:1]
        col_term[...] = grad_scale * (col_term[...] - t * cf[...])
        for n in range(4):
            for d in range(2):
                col_out[n][d] = col_term[pl.ds(pl.multiple_of(place[40 + n * 2 + d] * B, B), B), :]


def tile(place, rows, cols, accumulator):
    f32, bf16 = jnp.float32, jnp.bfloat16
    whole = pl.BlockSpec(memory_space=pltpu.VMEM)
    block = pl.BlockSpec((CHUNK, COLS), lambda i, place: (i, 0))
    pair = jax.ShapeDtypeStruct((2, B, F), f32)
    return pl.pallas_call(
        tile_kernel,
        out_shape=[jax.ShapeDtypeStruct((ROWS, COLS), f32)]
        + [pair] * 4
        + [jax.ShapeDtypeStruct((8, B, F), f32)]
        + [pair] * 4,
        grid_spec=pltpu.PrefetchScalarGridSpec(
            num_scalar_prefetch=1,
            grid=(STEPS,),
            in_specs=[whole] * 24 + [block],
            out_specs=[block] + [whole] * 9,
            scratch_shapes=[
                pltpu.VMEM((ROWS, F + K), bf16),
                pltpu.VMEM((ROWS, F + K), bf16),
                pltpu.VMEM((ROWS, F), f32),
                pltpu.VMEM((COLS, F + K), bf16),
                pltpu.VMEM((COLS, F + K), bf16),
                pltpu.VMEM((COLS, F), f32),
                pltpu.VMEM((ROWS, 128), f32),
                pltpu.VMEM((COLS, 128), f32),
                pltpu.VMEM((ROWS, F), f32),
                pltpu.VMEM((COLS, F), f32),
                pltpu.VMEM((8, COLS), f32),
            ],
        ),
        compiler_params=pltpu.CompilerParams(vmem_limit_bytes=46 * 1024 * 1024),
        cost_estimate=pl.CostEstimate(flops=8_000_000_000, bytes_accessed=20_000_000, transcendentals=524288),
        name="tile",
    )(place, *rows, *cols, accumulator)


def local(feat_rows, feat_cols, panel_rows, panel_cols, accumulator):
    q, r = lax.axis_index("col"), lax.axis_index("row")
    y, z, c = q // 8, (q // 2) % 4, q % 2
    x, h = r // 2, r % 2

    def row_at(dy, dz, dc):
        return (y ^ dy) * 8 + ((z + dz) % 4) * 2 + (c ^ dc)

    def col_at(dx, dh):
        return ((x + dx) % 4) * 2 + (h ^ dh)

    own_r = jnp.concatenate([feat_rows, panel_rows], axis=1)
    own_c = jnp.concatenate([feat_cols, panel_cols], axis=1)
    far_r = over_col(own_r, dy=1)
    far_c = over_row(own_c, dh=1)
    rows, cols = [], []
    for a_r, a_c in ((own_r, own_c), (far_r, far_c)):
        rows += [a_r] + [over_col(a_r, dz=-d) for d in SHIFTS[1:]]
        cols += [a_c] + [over_row(a_c, dx=-d) for d in SHIFTS[1:]]
    rows += [over_col(a, dc=1) for a in rows]
    place = jnp.stack(
        [row_at(dy, d, dc) for dc in range(2) for dy in range(2) for d in SHIFTS]
        + [col_at(d, dh) for dh in range(2) for d in SHIFTS]
        + [row_at(dy, d, dc) for dc in range(2) for d in SHIFTS for dy in range(2)]
        + [col_at(d, dh) for d in SHIFTS for dh in range(2)]
    ).astype(jnp.int32)
    out = tile(place, rows, cols, accumulator)
    acc_new, own, sib, col = out[0], out[1:5], out[5], out[6:10]
    sib = over_col(sib, dc=1)
    own = [a + sib[2 * n : 2 * n + 2] for n, a in enumerate(own)]
    row_sum, col_sum = own[0], col[0]
    for n in range(1, 4):
        row_sum = row_sum + over_col(own[n], dz=SHIFTS[n])
        col_sum = col_sum + over_row(col[n], dx=SHIFTS[n])
    grad_rows = row_sum[0] + over_col(row_sum[1], dy=1)
    grad_cols = col_sum[0] + over_row(col_sum[1], dh=1)
    return (acc_new, grad_rows, grad_cols)


def solution(mesh):
    in_specs = (
        P(("row", "col"), None),
        P(("col", "row"), None),
        P(("row", "col"), None),
        P(("col", "row"), None),
        P("row", "col"),
    )
    out_specs = (P("row", "col"), P(("row", "col"), None), P(("col", "row"), None))
    return jax.shard_map(local, mesh=mesh, in_specs=in_specs, out_specs=out_specs, check_vma=False)
```

```python
import jax
import jax.numpy as jnp
from jax import lax
from jax.experimental import pallas as pl
from jax.experimental.pallas import tpu as pltpu
from jax.sharding import PartitionSpec as P

decay_rate = 0.125
grad_scale = 0.25

B = 64
F = 512
K = 1024
STEPS = 4
ROWS = 1024
COLS = 512
CHUNK = ROWS // STEPS
SHIFTS = (0, 2, 1, 3)


def col_perm(dy, dz, dc):
    return [(q, (((q // 8) ^ dy) * 8) + (((q // 2 + dz) % 4) * 2) + ((q % 2) ^ dc)) for q in range(16)]


def row_perm(dx, dh):
    return [(r, ((r // 2 + dx) % 4) * 2 + ((r % 2) ^ dh)) for r in range(8)]


def over_col(a, dy=0, dz=0, dc=0):
    return lax.ppermute(a, "col", col_perm(dy, dz, dc))


def over_row(a, dx=0, dh=0):
    return lax.ppermute(a, "row", row_perm(dx, dh))


def split(a):
    hi = a.astype(jnp.bfloat16)
    return hi, (a - hi.astype(jnp.float32)).astype(jnp.bfloat16)


def dot3(ah, al, bh, bl, dims):
    def one(p, q):
        return lax.dot_general(p, q, (dims, ((), ())), preferred_element_type=jnp.float32)

    return one(ah, bh) + (one(ah, bl) + one(al, bh))


NT = ((1,), (1,))
NN = ((1,), (0,))
TN = ((0,), (0,))


f32, bf16 = jnp.float32, jnp.bfloat16
whole = pl.BlockSpec(memory_space=pltpu.VMEM)
block = pl.BlockSpec((CHUNK, COLS), lambda i: (i, 0))
W = F + K


def places():
    q, r = lax.axis_index("col"), lax.axis_index("row")
    y, z, c = q // 8, (q // 2) % 4, q % 2
    x, h = r // 2, r % 2

    def row_at(dy, dz, core):
        return (y ^ dy) * 8 + ((z + dz) % 4) * 2 + core

    def col_at(dx, dh):
        return ((x + dx) % 4) * 2 + (h ^ dh)

    return (
        [c]
        + [row_at(dy, d, 0) for dy in range(2) for d in SHIFTS]
        + [col_at(d, dh) for dh in range(2) for d in SHIFTS]
        + [row_at(dy, d, c) for d in SHIFTS for dy in range(2)]
        + [row_at(dy, d, 1 - c) for d in SHIFTS for dy in range(2)]
        + [col_at(d, dh) for d in SHIFTS for dh in range(2)]
    )


def pack_kernel(feat_rows, feat_cols, panel_rows, panel_cols, keep, give):
    def fill(mine, other):
        keep[:B, :F], keep[:B, F:] = mine[0][...], mine[1][...]
        give[:, :F], give[:, F:] = other[0][...], other[1][...]

    rows, cols = (feat_rows, panel_rows), (feat_cols, panel_cols)
    c = lax.axis_index("col") % 2
    pl.when(c == 0)(lambda: fill(rows, cols))
    pl.when(c == 1)(lambda: fill(cols, rows))


def pack(*shards):
    return pl.pallas_call(
        pack_kernel,
        out_shape=[jax.ShapeDtypeStruct((2 * B, W), f32), jax.ShapeDtypeStruct((B, W), f32)],
        in_specs=[whole] * 4,
        out_specs=[whole] * 2,
        compiler_params=pltpu.CompilerParams(vmem_limit_bytes=4 * 1024 * 1024),
        cost_estimate=pl.CostEstimate(flops=0, bytes_accessed=1_600_000, transcendentals=0),
        name="pack",
    )(*shards)


def tile_kernel(*refs):
    place = places()
    native, swapped, acc, acc_new = refs[:8], refs[8:16], refs[16], refs[17]
    own_out, sib_out, col_out = refs[18:22], refs[22], refs[23:27]
    rh, rl, rf, ch, cl, cf, nr, nc, row_term, col_term, tsum = refs[27:]
    step = pl.program_id(0)

    def put(a, at, hi, lo, feat, norm):
        hi[at, :], lo[at, :] = split(a)
        a = a[:, :F]
        feat[at, :] = a
        norm[at, :] = jnp.broadcast_to(jnp.sum(a * a, axis=1, keepdims=True), (a.shape[0], 128))

    @pl.when(step == 0)
    def _():
        def prepare(row_source, col_source, start):
            for n in range(8):
                at = pl.ds(pl.multiple_of(place[1 + n] * B, 2 * B), 2 * B)
                put(row_source[n][...], at, rh, rl, rf, nr)
                at = pl.ds(pl.multiple_of(place[9 + n] * B, B), B)
                put(col_source[n][start : start + B, :], at, ch, cl, cf, nc)

        pl.when(place[0] == 0)(lambda: prepare(native, swapped, B))
        pl.when(place[0] == 1)(lambda: prepare(swapped, native, 0))
        col_term[...] = jnp.zeros_like(col_term)
        tsum[...] = jnp.zeros_like(tsum)

    at = pl.ds(pl.multiple_of(step * CHUNK, CHUNK), CHUNK)
    grams = acc[...] + dot3(rh[at, F:], rl[at, F:], ch[:, F:], cl[:, F:], NT)
    acc_new[...] = grams
    cross = dot3(rh[at, :F], rl[at, :F], ch[:, :F], cl[:, :F], NT)
    nc_row = nc[...].T[0:1, :]
    dist_sq = nr[at, :][:, 0:1] + nc_row - 2.0 * cross
    weights = grams * jnp.exp(-decay_rate * dist_sq)
    wh, wl = split(weights)
    s = jnp.sum(weights, axis=1, keepdims=True)
    row_term[at, :] = grad_scale * (dot3(wh, wl, ch[:, :F], cl[:, :F], NN) - s * rf[at, :])
    col_term[...] += dot3(wh, wl, rh[at, :F], rl[at, :F], TN)
    tsum[...] += jnp.broadcast_to(jnp.sum(weights, axis=0, keepdims=True), (8, COLS))

    @pl.when(step == STEPS - 1)
    def _():
        def take(k, src):
            return src[pl.ds(pl.multiple_of(place[17 + k] * B, B), B), :]

        t = jnp.broadcast_to(tsum[0:1, :], (128, COLS)).T[:, 0:1]
        col_term[...] = grad_scale * (col_term[...] - t * cf[...])
        for n in range(4):
            for d in range(2):
                k = n * 2 + d
                own_out[n][d] = take(k, row_term)
                sib_out[k] = take(8 + k, row_term)
                col_out[n][d] = take(16 + k, col_term)


def tile(native, swapped, accumulator):
    pair = jax.ShapeDtypeStruct((2, B, F), f32)
    return pl.pallas_call(
        tile_kernel,
        out_shape=[jax.ShapeDtypeStruct((ROWS, COLS), f32)]
        + [pair] * 4
        + [jax.ShapeDtypeStruct((8, B, F), f32)]
        + [pair] * 4,
        grid_spec=pl.GridSpec(
            grid=(STEPS,),
            in_specs=[whole] * 16 + [block],
            out_specs=[block] + [whole] * 9,
            scratch_shapes=[
                pltpu.VMEM((ROWS, W), bf16),
                pltpu.VMEM((ROWS, W), bf16),
                pltpu.VMEM((ROWS, F), f32),
                pltpu.VMEM((COLS, W), bf16),
                pltpu.VMEM((COLS, W), bf16),
                pltpu.VMEM((COLS, F), f32),
                pltpu.VMEM((ROWS, 128), f32),
                pltpu.VMEM((COLS, 128), f32),
                pltpu.VMEM((ROWS, F), f32),
                pltpu.VMEM((COLS, F), f32),
                pltpu.VMEM((8, COLS), f32),
            ],
        ),
        compiler_params=pltpu.CompilerParams(vmem_limit_bytes=TILE_VMEM * 1024 * 1024),
        cost_estimate=pl.CostEstimate(flops=8_000_000_000, bytes_accessed=20_000_000, transcendentals=524288),
        name="tile",
    )(*native, *swapped, accumulator)


TILE_VMEM = 36


def both_perm(flip, shift):
    pairs = []
    for r in range(8):
        for q in range(16):
            if q % 2 == 0:
                to = r * 16 + ((q // 8) ^ flip) * 8 + ((q // 2 + shift) % 4) * 2
            else:
                to = (((r // 2 + shift) % 4) * 2 + ((r % 2) ^ flip)) * 16 + q
            pairs.append((r * 16 + q, to))
    return pairs


def over_both(a, flip=0, shift=0):
    return lax.ppermute(a, ("row", "col"), both_perm(flip, shift))


def gather(shards):
    keep, give = pack(*shards)
    own = lax.dynamic_update_slice(keep, over_col(give, dc=1), (B, 0))
    far = over_both(own, flip=1)
    native = []
    for a in (own, far):
        native += [a] + [over_both(a, shift=-d) for d in SHIFTS[1:]]
    return native, [over_col(a, dc=1) for a in native]


def local(feat_rows, feat_cols, panel_rows, panel_cols, accumulator):
    native, swapped = gather((feat_rows, feat_cols, panel_rows, panel_cols))
    out = tile(native, swapped, accumulator)
    acc_new, own, sib, col = out[0], out[1:5], out[5], out[6:10]
    sib = over_col(sib, dc=1)
    own = [a + sib[2 * n : 2 * n + 2] for n, a in enumerate(own)]
    row_sum, col_sum = own[0], col[0]
    for n in range(1, 4):
        row_sum = row_sum + over_col(own[n], dz=SHIFTS[n])
        col_sum = col_sum + over_row(col[n], dx=SHIFTS[n])
    grad_rows = row_sum[0] + over_col(row_sum[1], dy=1)
    grad_cols = col_sum[0] + over_row(col_sum[1], dh=1)
    return (acc_new, grad_rows, grad_cols)


def solution(mesh):
    in_specs = (
        P(("row", "col"), None),
        P(("col", "row"), None),
        P(("row", "col"), None),
        P(("col", "row"), None),
        P("row", "col"),
    )
    out_specs = (P("row", "col"), P(("row", "col"), None), P(("col", "row"), None))
    return jax.shard_map(local, mesh=mesh, in_specs=in_specs, out_specs=out_specs, check_vma=False)
```

```python
import jax
import jax.numpy as jnp
from jax import lax
from jax.experimental import pallas as pl
from jax.experimental.pallas import tpu as pltpu
from jax.sharding import PartitionSpec as P

decay_rate = 0.125
grad_scale = 0.25

B = 64
F = 512
K = 1024
STEPS = 4
ROWS = 1024
COLS = 512
CHUNK = ROWS // STEPS
SHIFTS = (0, 2, 1, 3)


def col_perm(dy, dz, dc):
    return [(q, (((q // 8) ^ dy) * 8) + (((q // 2 + dz) % 4) * 2) + ((q % 2) ^ dc)) for q in range(16)]


def row_perm(dx, dh):
    return [(r, ((r // 2 + dx) % 4) * 2 + ((r % 2) ^ dh)) for r in range(8)]


def over_col(a, dy=0, dz=0, dc=0):
    return lax.ppermute(a, "col", col_perm(dy, dz, dc))


def over_row(a, dx=0, dh=0):
    return lax.ppermute(a, "row", row_perm(dx, dh))


def split(a):
    hi = a.astype(jnp.bfloat16)
    return hi, (a - hi.astype(jnp.float32)).astype(jnp.bfloat16)


def dot3(ah, al, bh, bl, dims):
    def one(p, q):
        return lax.dot_general(p, q, (dims, ((), ())), preferred_element_type=jnp.float32)

    return one(ah, bh) + (one(ah, bl) + one(al, bh))


NT = ((1,), (1,))
NN = ((1,), (0,))
TN = ((0,), (0,))


f32, bf16 = jnp.float32, jnp.bfloat16
whole = pl.BlockSpec(memory_space=pltpu.VMEM)
block = pl.BlockSpec((CHUNK, COLS), lambda i: (i, 0))
W = F + K


def places():
    q, r = lax.axis_index("col"), lax.axis_index("row")
    y, z, c = q // 8, (q // 2) % 4, q % 2
    x, h = r // 2, r % 2

    def row_at(dy, dz, core):
        return (y ^ dy) * 8 + ((z + dz) % 4) * 2 + core

    def col_at(dx, dh):
        return ((x + dx) % 4) * 2 + (h ^ dh)

    return (
        [c]
        + [row_at(dy, d, 0) for dy in range(2) for d in SHIFTS]
        + [col_at(d, dh) for dh in range(2) for d in SHIFTS]
        + [row_at(dy, d, c) for d in SHIFTS for dy in range(2)]
        + [row_at(dy, d, 1 - c) for d in SHIFTS for dy in range(2)]
        + [col_at(d, dh) for d in SHIFTS for dh in range(2)]
    )


anywhere = pl.BlockSpec(memory_space=pl.ANY)


def pack_kernel(feat_rows, feat_cols, panel_rows, panel_cols, keep, give, sems):
    def copies(mine, other):
        return [
            pltpu.make_async_copy(other[0], give.at[:, :F], sems.at[0]),
            pltpu.make_async_copy(other[1], give.at[:, F:], sems.at[1]),
            pltpu.make_async_copy(mine[0], keep.at[:B, :F], sems.at[2]),
            pltpu.make_async_copy(mine[1], keep.at[:B, F:], sems.at[3]),
        ]

    rows, cols = (feat_rows, panel_rows), (feat_cols, panel_cols)

    def start(mine, other):
        for copy in copies(mine, other):
            copy.start()

    c = lax.axis_index("col") % 2
    pl.when(c == 0)(lambda: start(rows, cols))
    pl.when(c == 1)(lambda: start(cols, rows))
    for copy in copies(rows, cols):
        copy.wait()


def pack(*shards):
    return pl.pallas_call(
        pack_kernel,
        out_shape=[jax.ShapeDtypeStruct((2 * B, W), f32), jax.ShapeDtypeStruct((B, W), f32)],
        in_specs=[anywhere] * 4,
        out_specs=[whole] * 2,
        scratch_shapes=[pltpu.SemaphoreType.DMA((4,))],
        compiler_params=pltpu.CompilerParams(vmem_limit_bytes=PACK_VMEM * 1024 * 1024),
        cost_estimate=pl.CostEstimate(flops=0, bytes_accessed=1_600_000, transcendentals=0),
        name="pack",
    )(*shards)


PACK_VMEM = 4


def tile_kernel(*refs):
    place = places()
    native, swapped, acc, acc_new = refs[:9], refs[9:18], refs[18], refs[19]
    own_out, sib_out, col_out = refs[20:24], refs[24], refs[25:29]
    rh, rl, rf, ch, cl, cf, nr, nc, row_term, col_term, tsum = refs[29:]
    step = pl.program_id(0)

    def put(a, at, hi, lo, feat, norm):
        hi[at, :], lo[at, :] = split(a)
        a = a[:, :F]
        feat[at, :] = a
        norm[at, :] = jnp.broadcast_to(jnp.sum(a * a, axis=1, keepdims=True), (a.shape[0], 128))

    @pl.when(step == 0)
    def _():
        def prepare(row_source, col_source, start):
            for n in range(8):
                at = place[1 + n] * B
                col_at = pl.ds(pl.multiple_of(place[9 + n] * B, B), B)
                if n == HALVED:
                    for half in range(2):
                        put(row_source[n + half][...], pl.ds(pl.multiple_of(at + half * B, B), B), rh, rl, rf, nr)
                    put(col_source[n + start // B][...], col_at, ch, cl, cf, nc)
                    continue
                k = n + (n > HALVED)
                put(row_source[k][...], pl.ds(pl.multiple_of(at, 2 * B), 2 * B), rh, rl, rf, nr)
                put(col_source[k][start : start + B, :], col_at, ch, cl, cf, nc)

        pl.when(place[0] == 0)(lambda: prepare(native, swapped, B))
        pl.when(place[0] == 1)(lambda: prepare(swapped, native, 0))
        col_term[...] = jnp.zeros_like(col_term)
        tsum[...] = jnp.zeros_like(tsum)

    at = pl.ds(pl.multiple_of(step * CHUNK, CHUNK), CHUNK)
    grams = acc[...] + dot3(rh[at, F:], rl[at, F:], ch[:, F:], cl[:, F:], NT)
    acc_new[...] = grams
    cross = dot3(rh[at, :F], rl[at, :F], ch[:, :F], cl[:, :F], NT)
    nc_row = nc[...].T[0:1, :]
    dist_sq = nr[at, :][:, 0:1] + nc_row - 2.0 * cross
    weights = grams * jnp.exp(-decay_rate * dist_sq)
    wh, wl = split(weights)
    s = jnp.sum(weights, axis=1, keepdims=True)
    row_term[at, :] = grad_scale * (dot3(wh, wl, ch[:, :F], cl[:, :F], NN) - s * rf[at, :])
    col_term[...] += dot3(wh, wl, rh[at, :F], rl[at, :F], TN)
    tsum[...] += jnp.broadcast_to(jnp.sum(weights, axis=0, keepdims=True), (8, COLS))

    @pl.when(step == STEPS - 1)
    def _():
        def take(k, src):
            return src[pl.ds(pl.multiple_of(place[17 + k] * B, B), B), :]

        t = jnp.broadcast_to(tsum[0:1, :], (128, COLS)).T[:, 0:1]
        col_term[...] = grad_scale * (col_term[...] - t * cf[...])
        for n in range(4):
            for d in range(2):
                k = n * 2 + d
                own_out[n][d] = take(k, row_term)
                sib_out[k] = take(8 + k, row_term)
                col_out[n][d] = take(16 + k, col_term)


def tile(native, swapped, accumulator):
    pair = jax.ShapeDtypeStruct((2, B, F), f32)
    return pl.pallas_call(
        tile_kernel,
        out_shape=[jax.ShapeDtypeStruct((ROWS, COLS), f32)]
        + [pair] * 4
        + [jax.ShapeDtypeStruct((8, B, F), f32)]
        + [pair] * 4,
        grid_spec=pl.GridSpec(
            grid=(STEPS,),
            in_specs=[whole] * 18 + [block],
            out_specs=[block] + [whole] * 9,
            scratch_shapes=[
                pltpu.VMEM((ROWS, W), bf16),
                pltpu.VMEM((ROWS, W), bf16),
                pltpu.VMEM((ROWS, F), f32),
                pltpu.VMEM((COLS, W), bf16),
                pltpu.VMEM((COLS, W), bf16),
                pltpu.VMEM((COLS, F), f32),
                pltpu.VMEM((ROWS, 128), f32),
                pltpu.VMEM((COLS, 128), f32),
                pltpu.VMEM((ROWS, F), f32),
                pltpu.VMEM((COLS, F), f32),
                pltpu.VMEM((8, COLS), f32),
            ],
        ),
        compiler_params=pltpu.CompilerParams(vmem_limit_bytes=TILE_VMEM * 1024 * 1024),
        cost_estimate=pl.CostEstimate(flops=8_000_000_000, bytes_accessed=20_000_000, transcendentals=524288),
        name="tile",
    )(*native, *swapped, accumulator)


TILE_VMEM = 36


def both_perm(flip, shift):
    pairs = []
    for r in range(8):
        for q in range(16):
            if q % 2 == 0:
                to = r * 16 + ((q // 8) ^ flip) * 8 + ((q // 2 + shift) % 4) * 2
            else:
                to = (((r // 2 + shift) % 4) * 2 + ((r % 2) ^ flip)) * 16 + q
            pairs.append((r * 16 + q, to))
    return pairs


def over_both(a, flip=0, shift=0):
    return lax.ppermute(a, ("row", "col"), both_perm(flip, shift))


HALVED = 5


def gather(shards):
    keep, give = pack(*shards)
    own = lax.dynamic_update_slice(keep, over_col(give, dc=1), (B, 0))
    far = over_both(own, flip=1)
    near = [own] + [over_both(own, shift=-d) for d in SHIFTS[1:]]
    other = [far] + [over_both(far, shift=-d) for d in SHIFTS[2:]]
    halves = [over_both(far[:B], shift=-SHIFTS[1]), over_both(near[1][B:], flip=1)]
    native = near + other[:1] + halves + other[1:]
    return native, [over_col(a, dc=1) for a in native]


def local(feat_rows, feat_cols, panel_rows, panel_cols, accumulator):
    native, swapped = gather((feat_rows, feat_cols, panel_rows, panel_cols))
    out = tile(native, swapped, accumulator)
    acc_new, own, sib, col = out[0], out[1:5], out[5], out[6:10]
    sib = over_col(sib, dc=1)
    own = [a + sib[2 * n : 2 * n + 2] for n, a in enumerate(own)]
    row_sum, col_sum = own[0], col[0]
    for n in range(1, 4):
        row_sum = row_sum + over_col(own[n], dz=SHIFTS[n])
        col_sum = col_sum + over_row(col[n], dx=SHIFTS[n])
    grad_rows = row_sum[0] + over_col(row_sum[1], dy=1)
    grad_cols = col_sum[0] + over_row(col_sum[1], dh=1)
    return (acc_new, grad_rows, grad_cols)


def solution(mesh):
    in_specs = (
        P(("row", "col"), None),
        P(("col", "row"), None),
        P(("row", "col"), None),
        P(("col", "row"), None),
        P("row", "col"),
    )
    out_specs = (P("row", "col"), P(("row", "col"), None), P(("col", "row"), None))
    return jax.shard_map(local, mesh=mesh, in_specs=in_specs, out_specs=out_specs, check_vma=False)
```

```python
import jax
import jax.numpy as jnp
from jax import lax
from jax.experimental import pallas as pl
from jax.experimental.pallas import tpu as pltpu
from jax.sharding import PartitionSpec as P

decay_rate = 0.125
grad_scale = 0.25

B = 64
F = 512
K = 1024
STEPS = 1
ROWS = 1024
COLS = 512
CHUNK = ROWS // STEPS
SHIFTS = (0, 2, 1, 3)


def col_perm(dy, dz, dc):
    return [(q, (((q // 8) ^ dy) * 8) + (((q // 2 + dz) % 4) * 2) + ((q % 2) ^ dc)) for q in range(16)]


def row_perm(dx, dh):
    return [(r, ((r // 2 + dx) % 4) * 2 + ((r % 2) ^ dh)) for r in range(8)]


def over_col(a, dy=0, dz=0, dc=0):
    return lax.ppermute(a, "col", col_perm(dy, dz, dc))


def over_row(a, dx=0, dh=0):
    return lax.ppermute(a, "row", row_perm(dx, dh))


def split(a):
    hi = a.astype(jnp.bfloat16)
    return hi, (a - hi.astype(jnp.float32)).astype(jnp.bfloat16)


def dot3(ah, al, bh, bl, dims):
    def one(p, q):
        return lax.dot_general(p, q, (dims, ((), ())), preferred_element_type=jnp.float32)

    return one(ah, bh) + (one(ah, bl) + one(al, bh))


NT = ((1,), (1,))
NN = ((1,), (0,))
TN = ((0,), (0,))


f32, bf16 = jnp.float32, jnp.bfloat16
whole = pl.BlockSpec(memory_space=pltpu.VMEM)
block = pl.BlockSpec((CHUNK, COLS), lambda i: (i, 0))
W = F + K


def places():
    q, r = lax.axis_index("col"), lax.axis_index("row")
    y, z, c = q // 8, (q // 2) % 4, q % 2
    x, h = r // 2, r % 2

    def row_at(dy, dz, core):
        return (y ^ dy) * 8 + ((z + dz) % 4) * 2 + core

    def col_at(dx, dh):
        return ((x + dx) % 4) * 2 + (h ^ dh)

    return (
        [c]
        + [row_at(dy, d, 0) for dy in range(2) for d in SHIFTS]
        + [col_at(d, dh) for dh in range(2) for d in SHIFTS]
        + [row_at(dy, d, c) for d in SHIFTS for dy in range(2)]
        + [row_at(dy, d, 1 - c) for d in SHIFTS for dy in range(2)]
        + [col_at(d, dh) for d in SHIFTS for dh in range(2)]
    )


anywhere = pl.BlockSpec(memory_space=pl.ANY)


def pack_kernel(feat_rows, feat_cols, panel_rows, panel_cols, keep, give, sems):
    def copies(mine, other):
        return [
            pltpu.make_async_copy(other[0], give.at[:, :F], sems.at[0]),
            pltpu.make_async_copy(other[1], give.at[:, F:], sems.at[1]),
            pltpu.make_async_copy(mine[0], keep.at[:B, :F], sems.at[2]),
            pltpu.make_async_copy(mine[1], keep.at[:B, F:], sems.at[3]),
        ]

    rows, cols = (feat_rows, panel_rows), (feat_cols, panel_cols)

    def start(mine, other):
        for copy in copies(mine, other):
            copy.start()

    c = lax.axis_index("col") % 2
    pl.when(c == 0)(lambda: start(rows, cols))
    pl.when(c == 1)(lambda: start(cols, rows))
    for copy in copies(rows, cols):
        copy.wait()


def pack(*shards):
    return pl.pallas_call(
        pack_kernel,
        out_shape=[jax.ShapeDtypeStruct((2 * B, W), f32), jax.ShapeDtypeStruct((B, W), f32)],
        in_specs=[anywhere] * 4,
        out_specs=[whole] * 2,
        scratch_shapes=[pltpu.SemaphoreType.DMA((4,))],
        compiler_params=pltpu.CompilerParams(vmem_limit_bytes=PACK_VMEM * 1024 * 1024),
        cost_estimate=pl.CostEstimate(flops=0, bytes_accessed=1_600_000, transcendentals=0),
        name="pack",
    )(*shards)


PACK_VMEM = 4


def tile_kernel(*refs):
    place = places()
    native, swapped, acc, acc_new = refs[:9], refs[9:18], refs[18], refs[19]
    own_out, sib_out, col_out = refs[20:24], refs[24], refs[25:29]
    rh, rl, rf, ch, cl, cf, nr, nc, row_term, col_term, tsum = refs[29:]
    step = pl.program_id(0)

    def put(a, at, hi, lo, feat, norm):
        hi[at, :], lo[at, :] = split(a)
        a = a[:, :F]
        feat[at, :] = a
        norm[at, :] = jnp.broadcast_to(jnp.sum(a * a, axis=1, keepdims=True), (a.shape[0], 128))

    @pl.when(step == 0)
    def _():
        def prepare(row_source, col_source, start):
            for n in range(8):
                at = place[1 + n] * B
                col_at = pl.ds(pl.multiple_of(place[9 + n] * B, B), B)
                if n == HALVED:
                    for half in range(2):
                        put(row_source[n + half][...], pl.ds(pl.multiple_of(at + half * B, B), B), rh, rl, rf, nr)
                    put(col_source[n + start // B][...], col_at, ch, cl, cf, nc)
                    continue
                k = n + (n > HALVED)
                put(row_source[k][...], pl.ds(pl.multiple_of(at, 2 * B), 2 * B), rh, rl, rf, nr)
                put(col_source[k][start : start + B, :], col_at, ch, cl, cf, nc)

        pl.when(place[0] == 0)(lambda: prepare(native, swapped, B))
        pl.when(place[0] == 1)(lambda: prepare(swapped, native, 0))
        col_term[...] = jnp.zeros_like(col_term)
        tsum[...] = jnp.zeros_like(tsum)

    at = pl.ds(pl.multiple_of(step * CHUNK, CHUNK), CHUNK)
    grams = acc[...] + dot3(rh[at, F:], rl[at, F:], ch[:, F:], cl[:, F:], NT)
    acc_new[...] = grams
    cross = dot3(rh[at, :F], rl[at, :F], ch[:, :F], cl[:, :F], NT)
    nc_row = nc[...].T[0:1, :]
    dist_sq = nr[at, :][:, 0:1] + nc_row - 2.0 * cross
    weights = grams * jnp.exp(-decay_rate * dist_sq)
    wh, wl = split(weights)
    s = jnp.sum(weights, axis=1, keepdims=True)
    row_term[at, :] = grad_scale * (dot3(wh, wl, ch[:, :F], cl[:, :F], NN) - s * rf[at, :])
    col_term[...] += dot3(wh, wl, rh[at, :F], rl[at, :F], TN)
    tsum[...] += jnp.broadcast_to(jnp.sum(weights, axis=0, keepdims=True), (8, COLS))

    @pl.when(step == STEPS - 1)
    def _():
        def take(k, src):
            return src[pl.ds(pl.multiple_of(place[17 + k] * B, B), B), :]

        t = jnp.broadcast_to(tsum[0:1, :], (128, COLS)).T[:, 0:1]
        col_term[...] = grad_scale * (col_term[...] - t * cf[...])
        for n in range(4):
            for d in range(2):
                k = n * 2 + d
                own_out[n][d] = take(k, row_term)
                sib_out[k] = take(8 + k, row_term)
                col_out[n][d] = take(16 + k, col_term)


def tile(native, swapped, accumulator):
    pair = jax.ShapeDtypeStruct((2, B, F), f32)
    return pl.pallas_call(
        tile_kernel,
        out_shape=[jax.ShapeDtypeStruct((ROWS, COLS), f32)]
        + [pair] * 4
        + [jax.ShapeDtypeStruct((8, B, F), f32)]
        + [pair] * 4,
        grid_spec=pl.GridSpec(
            grid=(STEPS,),
            in_specs=[whole] * 18 + [block],
            out_specs=[block] + [whole] * 9,
            scratch_shapes=[
                pltpu.VMEM((ROWS, W), bf16),
                pltpu.VMEM((ROWS, W), bf16),
                pltpu.VMEM((ROWS, F), f32),
                pltpu.VMEM((COLS, W), bf16),
                pltpu.VMEM((COLS, W), bf16),
                pltpu.VMEM((COLS, F), f32),
                pltpu.VMEM((ROWS, 128), f32),
                pltpu.VMEM((COLS, 128), f32),
                pltpu.VMEM((ROWS, F), f32),
                pltpu.VMEM((COLS, F), f32),
                pltpu.VMEM((8, COLS), f32),
            ],
        ),
        compiler_params=pltpu.CompilerParams(vmem_limit_bytes=TILE_VMEM * 1024 * 1024),
        cost_estimate=pl.CostEstimate(flops=8_000_000_000, bytes_accessed=20_000_000, transcendentals=524288),
        name="tile",
    )(*native, *swapped, accumulator)


TILE_VMEM = 36


def both_perm(flip, shift):
    pairs = []
    for r in range(8):
        for q in range(16):
            if q % 2 == 0:
                to = r * 16 + ((q // 8) ^ flip) * 8 + ((q // 2 + shift) % 4) * 2
            else:
                to = (((r // 2 + shift) % 4) * 2 + ((r % 2) ^ flip)) * 16 + q
            pairs.append((r * 16 + q, to))
    return pairs


def over_both(a, flip=0, shift=0):
    return lax.ppermute(a, ("row", "col"), both_perm(flip, shift))


HALVED = 5


def gather(shards):
    keep, give = pack(*shards)
    own = lax.dynamic_update_slice(keep, over_col(give, dc=1), (B, 0))
    far = over_both(own, flip=1)
    near = [own] + [over_both(own, shift=-d) for d in SHIFTS[1:]]
    other = [far] + [over_both(far, shift=-d) for d in SHIFTS[2:]]
    halves = [over_both(far[:B], shift=-SHIFTS[1]), over_both(near[1][B:], flip=1)]
    native = near + other[:1] + halves + other[1:]
    return native, [over_col(a, dc=1) for a in native]


def local(feat_rows, feat_cols, panel_rows, panel_cols, accumulator):
    native, swapped = gather((feat_rows, feat_cols, panel_rows, panel_cols))
    out = tile(native, swapped, accumulator)
    acc_new, own, sib, col = out[0], out[1:5], out[5], out[6:10]
    sib = over_col(sib, dc=1)
    own = [a + sib[2 * n : 2 * n + 2] for n, a in enumerate(own)]
    row_sum, col_sum = own[0], col[0]
    for n in range(1, 4):
        row_sum = row_sum + over_col(own[n], dz=SHIFTS[n])
        col_sum = col_sum + over_row(col[n], dx=SHIFTS[n])
    grad_rows = row_sum[0] + over_col(row_sum[1], dy=1)
    grad_cols = col_sum[0] + over_row(col_sum[1], dh=1)
    return (acc_new, grad_rows, grad_cols)


def solution(mesh):
    in_specs = (
        P(("row", "col"), None),
        P(("col", "row"), None),
        P(("row", "col"), None),
        P(("col", "row"), None),
        P("row", "col"),
    )
    out_specs = (P("row", "col"), P(("row", "col"), None), P(("col", "row"), None))
    return jax.shard_map(local, mesh=mesh, in_specs=in_specs, out_specs=out_specs, check_vma=False)
```

```python
import jax
import jax.numpy as jnp
from jax import lax
from jax.experimental import pallas as pl
from jax.experimental.pallas import tpu as pltpu
from jax.sharding import PartitionSpec as P

decay_rate = 0.125
grad_scale = 0.25

B = 64
F = 512
K = 1024
ROWS = 1024
COLS = 512
SHIFTS = (0, 2, 1, 3)


def col_perm(dy, dz, dc):
    return [(q, (((q // 8) ^ dy) * 8) + (((q // 2 + dz) % 4) * 2) + ((q % 2) ^ dc)) for q in range(16)]


def row_perm(dx, dh):
    return [(r, ((r // 2 + dx) % 4) * 2 + ((r % 2) ^ dh)) for r in range(8)]


def over_col(a, dy=0, dz=0, dc=0):
    return lax.ppermute(a, "col", col_perm(dy, dz, dc))


def over_row(a, dx=0, dh=0):
    return lax.ppermute(a, "row", row_perm(dx, dh))


def split(a):
    hi = a.astype(jnp.bfloat16)
    return hi, (a - hi.astype(jnp.float32)).astype(jnp.bfloat16)


def dot3(ah, al, bh, bl, dims):
    def one(p, q):
        return lax.dot_general(p, q, (dims, ((), ())), preferred_element_type=jnp.float32)

    return one(ah, bh) + (one(ah, bl) + one(al, bh))


NT = ((1,), (1,))
NN = ((1,), (0,))
TN = ((0,), (0,))


f32, bf16 = jnp.float32, jnp.bfloat16
whole = pl.BlockSpec(memory_space=pltpu.VMEM)
W = F + K


def places():
    q, r = lax.axis_index("col"), lax.axis_index("row")
    y, z, c = q // 8, (q // 2) % 4, q % 2
    x, h = r // 2, r % 2

    def row_at(dy, dz, core):
        return (y ^ dy) * 8 + ((z + dz) % 4) * 2 + core

    def col_at(dx, dh):
        return ((x + dx) % 4) * 2 + (h ^ dh)

    return (
        [c]
        + [row_at(dy, d, 0) for dy in range(2) for d in SHIFTS]
        + [col_at(d, dh) for dh in range(2) for d in SHIFTS]
        + [row_at(dy, d, c) for d in SHIFTS for dy in range(2)]
        + [row_at(dy, d, 1 - c) for d in SHIFTS for dy in range(2)]
        + [col_at(d, dh) for d in SHIFTS for dh in range(2)]
    )


anywhere = pl.BlockSpec(memory_space=pl.ANY)


def pack_kernel(feat_rows, feat_cols, panel_rows, panel_cols, keep, give, sems):
    def copies(mine, other):
        return [
            pltpu.make_async_copy(other[0], give.at[:, :F], sems.at[0]),
            pltpu.make_async_copy(other[1], give.at[:, F:], sems.at[1]),
            pltpu.make_async_copy(mine[0], keep.at[:, :F], sems.at[2]),
            pltpu.make_async_copy(mine[1], keep.at[:, F:], sems.at[3]),
        ]

    rows, cols = (feat_rows, panel_rows), (feat_cols, panel_cols)

    def start(mine, other):
        for copy in copies(mine, other):
            copy.start()

    c = lax.axis_index("col") % 2
    pl.when(c == 0)(lambda: start(rows, cols))
    pl.when(c == 1)(lambda: start(cols, rows))
    for copy in copies(rows, cols):
        copy.wait()


def pack(*shards):
    return pl.pallas_call(
        pack_kernel,
        out_shape=[jax.ShapeDtypeStruct((B, W), f32)] * 2,
        in_specs=[anywhere] * 4,
        out_specs=[whole] * 2,
        scratch_shapes=[pltpu.SemaphoreType.DMA((4,))],
        compiler_params=pltpu.CompilerParams(vmem_limit_bytes=PACK_VMEM * 1024 * 1024),
        cost_estimate=pl.CostEstimate(flops=0, bytes_accessed=1_600_000, transcendentals=0),
        name="pack",
    )(*shards)


PACK_VMEM = 60


def put(a, at, hi, lo, norm):
    hi[at, :], lo[at, :] = split(a)
    a = a[:, :F]
    norm[at, :] = jnp.broadcast_to(jnp.sum(a * a, axis=1, keepdims=True), (a.shape[0], 128))


def tile_kernel(*refs):
    native, swapped, acc, acc_new = refs[:9], refs[9:18], refs[18], refs[19]
    own_out, sib_out, col_out = refs[20:24], refs[24], refs[25:29]
    rh, rl, nr, ch, cl, nc, row_term, col_term = refs[29:]
    place = places()
    def prepare(row_source, col_source, start):
        for n in range(8):
            k = n + (n > HALVED)
            at = place[1 + n] * B
            col_at = pl.ds(pl.multiple_of(place[9 + n] * B, B), B)
            if n == HALVED:
                for half in range(2):
                    put(row_source[k + half][...], pl.ds(pl.multiple_of(at + half * B, B), B), rh, rl, nr)
                put(col_source[k + start // B][...], col_at, ch, cl, nc)
                continue
            put(row_source[k][...], pl.ds(pl.multiple_of(at, 2 * B), 2 * B), rh, rl, nr)
            put(col_source[k][start : start + B, :], col_at, ch, cl, nc)

    pl.when(place[0] == 0)(lambda: prepare(native, swapped, B))
    pl.when(place[0] == 1)(lambda: prepare(swapped, native, 0))

    def feat(hi, lo):
        return hi[:, :F].astype(f32) + lo[:, :F].astype(f32)

    grams = acc[...] + dot3(rh[:, F:], rl[:, F:], ch[:, F:], cl[:, F:], NT)
    acc_new[...] = grams
    cross = dot3(rh[:, :F], rl[:, :F], ch[:, :F], cl[:, :F], NT)
    nc_row = nc[...].T[0:1, :]
    dist_sq = nr[:, 0:1] + nc_row - 2.0 * cross
    weights = grams * jnp.exp(-decay_rate * dist_sq)
    wh, wl = split(weights)
    s = jnp.sum(weights, axis=1, keepdims=True)
    row_term[...] = grad_scale * (dot3(wh, wl, ch[:, :F], cl[:, :F], NN) - s * feat(rh, rl))
    t = jnp.broadcast_to(jnp.sum(weights, axis=0, keepdims=True), (128, COLS)).T[:, 0:1]
    col_term[...] = grad_scale * (dot3(wh, wl, rh[:, :F], rl[:, :F], TN) - t * feat(ch, cl))

    def take(k, src):
        return src[pl.ds(pl.multiple_of(place[17 + k] * B, B), B), :]

    for n in range(4):
        for d in range(2):
            k = n * 2 + d
            own_out[n][d] = take(k, row_term)
            sib_out[k] = take(8 + k, row_term)
            col_out[n][d] = take(16 + k, col_term)


def tile(native, swapped, accumulator):
    pair = jax.ShapeDtypeStruct((2, B, F), f32)
    return pl.pallas_call(
        tile_kernel,
        out_shape=[jax.ShapeDtypeStruct((ROWS, COLS), f32)]
        + [pair] * 4
        + [jax.ShapeDtypeStruct((8, B, F), f32)]
        + [pair] * 4,
        in_specs=[whole] * 19,
        out_specs=[whole] * 10,
        scratch_shapes=[
            pltpu.VMEM((ROWS, W), bf16),
            pltpu.VMEM((ROWS, W), bf16),
            pltpu.VMEM((ROWS, 128), f32),
            pltpu.VMEM((COLS, W), bf16),
            pltpu.VMEM((COLS, W), bf16),
            pltpu.VMEM((COLS, 128), f32),
            pltpu.VMEM((ROWS, F), f32),
            pltpu.VMEM((COLS, F), f32),
        ],
        compiler_params=pltpu.CompilerParams(vmem_limit_bytes=TILE_VMEM * 1024 * 1024),
        cost_estimate=pl.CostEstimate(flops=8_000_000_000, bytes_accessed=20_000_000, transcendentals=524288),
        name="tile",
    )(*native, *swapped, accumulator)


TILE_VMEM = 36


def both_perm(flip, shift):
    pairs = []
    for r in range(8):
        for q in range(16):
            if q % 2 == 0:
                to = r * 16 + ((q // 8) ^ flip) * 8 + ((q // 2 + shift) % 4) * 2
            else:
                to = (((r // 2 + shift) % 4) * 2 + ((r % 2) ^ flip)) * 16 + q
            pairs.append((r * 16 + q, to))
    return pairs


def over_both(a, flip=0, shift=0):
    return lax.ppermute(a, ("row", "col"), both_perm(flip, shift))


HALVED = 5


def gather(shards):
    keep, give = pack(*shards)
    own = jnp.concatenate([keep, over_col(give, dc=1)], axis=0)
    far = over_both(own, flip=1)
    near = [own] + [over_both(own, shift=-d) for d in SHIFTS[1:]]
    other = [far] + [over_both(far, shift=-d) for d in SHIFTS[2:]]
    halves = [over_both(far[:B], shift=-SHIFTS[1]), over_both(near[1][B:], flip=1)]
    native = near + other[:1] + halves + other[1:]
    return native, [over_col(a, dc=1) for a in native]


def local(feat_rows, feat_cols, panel_rows, panel_cols, accumulator):
    native, swapped = gather((feat_rows, feat_cols, panel_rows, panel_cols))
    out = tile(native, swapped, accumulator)
    acc_new, own, sib, col = out[0], out[1:5], out[5], out[6:10]
    sib = over_col(sib, dc=1)
    own = [a + sib[2 * n : 2 * n + 2] for n, a in enumerate(own)]
    row_sum, col_sum = own[0], col[0]
    for n in range(1, 4):
        row_sum = row_sum + over_col(own[n], dz=SHIFTS[n])
        col_sum = col_sum + over_row(col[n], dx=SHIFTS[n])
    grad_rows = row_sum[0] + over_col(row_sum[1], dy=1)
    grad_cols = col_sum[0] + over_row(col_sum[1], dh=1)
    return (acc_new, grad_rows, grad_cols)


def solution(mesh):
    in_specs = (
        P(("row", "col"), None),
        P(("col", "row"), None),
        P(("row", "col"), None),
        P(("col", "row"), None),
        P("row", "col"),
    )
    out_specs = (P("row", "col"), P(("row", "col"), None), P(("col", "row"), None))
    return jax.shard_map(local, mesh=mesh, in_specs=in_specs, out_specs=out_specs, check_vma=False)
```

```python
import jax
import jax.numpy as jnp
from jax import lax
from jax.experimental import pallas as pl
from jax.experimental.pallas import tpu as pltpu
from jax.sharding import PartitionSpec as P

decay_rate = 0.125
grad_scale = 0.25

B = 64
F = 512
K = 1024
ROWS = 1024
COLS = 512
SHIFTS = (0, 2, 1, 3)


def col_perm(dy, dz, dc):
    return [(q, (((q // 8) ^ dy) * 8) + (((q // 2 + dz) % 4) * 2) + ((q % 2) ^ dc)) for q in range(16)]


def row_perm(dx, dh):
    return [(r, ((r // 2 + dx) % 4) * 2 + ((r % 2) ^ dh)) for r in range(8)]


def over_col(a, dy=0, dz=0, dc=0):
    return lax.ppermute(a, "col", col_perm(dy, dz, dc))


def over_row(a, dx=0, dh=0):
    return lax.ppermute(a, "row", row_perm(dx, dh))


def split(a):
    hi = a.astype(jnp.bfloat16)
    return hi, (a - hi.astype(jnp.float32)).astype(jnp.bfloat16)


def dot3(ah, al, bh, bl, dims):
    def one(p, q):
        return lax.dot_general(p, q, (dims, ((), ())), preferred_element_type=jnp.float32)

    return one(ah, bh) + (one(ah, bl) + one(al, bh))


NT = ((1,), (1,))
NN = ((1,), (0,))
TN = ((0,), (0,))


f32, bf16 = jnp.float32, jnp.bfloat16
whole = pl.BlockSpec(memory_space=pltpu.VMEM)
W = F + K


def places():
    q, r = lax.axis_index("col"), lax.axis_index("row")
    y, z, c = q // 8, (q // 2) % 4, q % 2
    x, h = r // 2, r % 2

    def row_at(dy, dz, core):
        return (y ^ dy) * 8 + ((z + dz) % 4) * 2 + core

    def col_at(dx, dh):
        return ((x + dx) % 4) * 2 + (h ^ dh)

    return (
        [c]
        + [row_at(dy, d, 0) for dy in range(2) for d in SHIFTS]
        + [col_at(d, dh) for dh in range(2) for d in SHIFTS]
        + [row_at(dy, d, c) for d in SHIFTS for dy in range(2)]
        + [row_at(dy, d, 1 - c) for d in SHIFTS for dy in range(2)]
        + [col_at(d, dh) for d in SHIFTS for dh in range(2)]
    )


anywhere = pl.BlockSpec(memory_space=pl.ANY)


def pack_kernel(feat_rows, feat_cols, panel_rows, panel_cols, keep, give, sems):
    def copies(mine, other):
        return [
            pltpu.make_async_copy(other[0], give.at[:, :F], sems.at[0]),
            pltpu.make_async_copy(other[1], give.at[:, F:], sems.at[1]),
            pltpu.make_async_copy(mine[0], keep.at[:, :F], sems.at[2]),
            pltpu.make_async_copy(mine[1], keep.at[:, F:], sems.at[3]),
        ]

    rows, cols = (feat_rows, panel_rows), (feat_cols, panel_cols)

    def start(mine, other):
        for copy in copies(mine, other):
            copy.start()

    c = lax.axis_index("col") % 2
    pl.when(c == 0)(lambda: start(rows, cols))
    pl.when(c == 1)(lambda: start(cols, rows))
    for copy in copies(rows, cols):
        copy.wait()


def pack(*shards):
    return pl.pallas_call(
        pack_kernel,
        out_shape=[jax.ShapeDtypeStruct((B, W), f32)] * 2,
        in_specs=[anywhere] * 4,
        out_specs=[whole] * 2,
        scratch_shapes=[pltpu.SemaphoreType.DMA((4,))],
        compiler_params=pltpu.CompilerParams(vmem_limit_bytes=PACK_VMEM * 1024 * 1024),
        cost_estimate=pl.CostEstimate(flops=0, bytes_accessed=1_600_000, transcendentals=0),
        name="pack",
    )(*shards)


PACK_VMEM = 60


def put(a, at, hi, lo, norm):
    hi[at, :], lo[at, :] = split(a)
    a = a[:, :F]
    norm[at, :] = jnp.broadcast_to(jnp.sum(a * a, axis=1, keepdims=True), (a.shape[0], 128))


def tile_kernel(*refs):
    native, swapped, acc, acc_new = refs[:9], refs[9:18], refs[18], refs[19]
    own_out, sib_out, col_out = refs[20:24], refs[24], refs[25:29]
    rh, rl, nr, ch, cl, nc, row_term, col_term = refs[29:]
    place = places()
    def prepare(row_source, col_source, start):
        for n in range(8):
            k = n + (n > HALVED)
            at = place[1 + n] * B
            col_at = pl.ds(pl.multiple_of(place[9 + n] * B, B), B)
            if n == HALVED:
                for half in range(2):
                    put(row_source[k + half][...], pl.ds(pl.multiple_of(at + half * B, B), B), rh, rl, nr)
                put(col_source[k + start // B][...], col_at, ch, cl, nc)
                continue
            put(row_source[k][...], pl.ds(pl.multiple_of(at, 2 * B), 2 * B), rh, rl, nr)
            put(col_source[k][start : start + B, :], col_at, ch, cl, nc)

    pl.when(place[0] == 0)(lambda: prepare(native, swapped, B))
    pl.when(place[0] == 1)(lambda: prepare(swapped, native, 0))

    def feat(hi, lo):
        return hi[:, :F].astype(f32) + lo[:, :F].astype(f32)

    grams = acc[...] + dot3(rh[:, F:], rl[:, F:], ch[:, F:], cl[:, F:], NT)
    acc_new[...] = grams
    cross = dot3(rh[:, :F], rl[:, :F], ch[:, :F], cl[:, :F], NT)
    nc_row = nc[...].T[0:1, :]
    dist_sq = nr[:, 0:1] + nc_row - 2.0 * cross
    weights = grams * jnp.exp(-decay_rate * dist_sq)
    wh, wl = split(weights)
    s = jnp.sum(weights, axis=1, keepdims=True)
    row_term[...] = grad_scale * (dot3(wh, wl, ch[:, :F], cl[:, :F], NN) - s * feat(rh, rl))
    t = jnp.broadcast_to(jnp.sum(weights, axis=0, keepdims=True), (128, COLS)).T[:, 0:1]
    col_term[...] = grad_scale * (dot3(wh, wl, rh[:, :F], rl[:, :F], TN) - t * feat(ch, cl))

    def take(k, src):
        return src[pl.ds(pl.multiple_of(place[17 + k] * B, B), B), :]

    for n in range(4):
        for d in range(2):
            k = n * 2 + d
            own_out[n][d] = take(k, row_term)
            sib_out[k] = take(8 + k, row_term)
            col_out[n][d] = take(16 + k, col_term)


def tile(native, swapped, accumulator):
    pair = jax.ShapeDtypeStruct((2, B, F), f32)
    return pl.pallas_call(
        tile_kernel,
        out_shape=[jax.ShapeDtypeStruct((ROWS, COLS), f32)]
        + [pair] * 4
        + [jax.ShapeDtypeStruct((8, B, F), f32)]
        + [pair] * 4,
        in_specs=[whole] * 19,
        out_specs=[whole] * 10,
        scratch_shapes=[
            pltpu.VMEM((ROWS, W), bf16),
            pltpu.VMEM((ROWS, W), bf16),
            pltpu.VMEM((ROWS, 128), f32),
            pltpu.VMEM((COLS, W), bf16),
            pltpu.VMEM((COLS, W), bf16),
            pltpu.VMEM((COLS, 128), f32),
            pltpu.VMEM((ROWS, F), f32),
            pltpu.VMEM((COLS, F), f32),
        ],
        compiler_params=pltpu.CompilerParams(vmem_limit_bytes=TILE_VMEM * 1024 * 1024),
        cost_estimate=pl.CostEstimate(flops=8_000_000_000, bytes_accessed=20_000_000, transcendentals=524288),
        name="tile",
    )(*native, *swapped, accumulator)


TILE_VMEM = 36


def both_perm(flip, shift):
    pairs = []
    for r in range(8):
        for q in range(16):
            if q % 2 == 0:
                to = r * 16 + ((q // 8) ^ flip) * 8 + ((q // 2 + shift) % 4) * 2
            else:
                to = (((r // 2 + shift) % 4) * 2 + ((r % 2) ^ flip)) * 16 + q
            pairs.append((r * 16 + q, to))
    return pairs


def over_both(a, flip=0, shift=0):
    return lax.ppermute(a, ("row", "col"), both_perm(flip, shift))


HALVED = 5


def gather(shards):
    keep, give = pack(*shards)
    own = jnp.concatenate([keep, over_col(give, dc=1)], axis=0)
    far = over_both(own, flip=1)
    near = [own] + [over_both(own, shift=-d) for d in SHIFTS[1:]]
    other = [far] + [over_both(far, shift=-d) for d in SHIFTS[2:]]
    halves = [over_both(far[:B], shift=-SHIFTS[1]), over_both(near[1][B:], flip=1)]
    native = near + other[:1] + halves + other[1:]
    return native, [over_col(a, dc=1) for a in native]


def local(feat_rows, feat_cols, panel_rows, panel_cols, accumulator):
    native, swapped = gather((feat_rows, feat_cols, panel_rows, panel_cols))
    out = tile(native, swapped, accumulator)
    acc_new, own, sib, col = out[0], out[1:5], out[5], out[6:10]
    sib = over_col(sib, dc=1)
    own = [a + sib[2 * n : 2 * n + 2] for n, a in enumerate(own)]
    row_sum, col_sum = own[0], col[0]
    for n in (1, 3, 2):
        row_sum = row_sum + over_col(own[n], dz=SHIFTS[n])
        col_sum = col_sum + over_row(col[n], dx=SHIFTS[n])
    grad_rows = row_sum[0] + over_col(row_sum[1], dy=1)
    grad_cols = col_sum[0] + over_row(col_sum[1], dh=1)
    return (acc_new, grad_rows, grad_cols)


def solution(mesh):
    in_specs = (
        P(("row", "col"), None),
        P(("col", "row"), None),
        P(("row", "col"), None),
        P(("col", "row"), None),
        P("row", "col"),
    )
    out_specs = (P("row", "col"), P(("row", "col"), None), P(("col", "row"), None))
    return jax.shard_map(local, mesh=mesh, in_specs=in_specs, out_specs=out_specs, check_vma=False)
```
